32 devices in a mesh: wide: 8 (over z, x), narrow: 4 (over y, core).
Axes of the slice: x: 2, y: 2, z: 4, core: 2. Of those that a mesh axis runs over, the one named last changes fastest.
Arguments:
- ensemble: bfloat16 [1024, 65536], P('narrow', 'wide'), may hold values from -6 to 6
- owner: int32 [512], P('wide'), may hold values from 0 to 63, as said below
- inflation: float32 [64], replicated, may hold values from 1 to 2
- obs_block: int32 [128], P('wide'), may hold values from 0 to 63
- obs_value: float32 [16384], P('wide'), may hold values from -12 to 12
- obs_std: float32 [16384], P('wide'), may hold values from 1 to 300
Outputs:
- analysis: bfloat16 [1024, 65536], P('narrow', 'wide')
The draws below stay inside these ranges and needn't reach their ends.
Inputs may be any that keep to these rules, and one draw needn't show every extreme that they name: `obs_block`: indexes one of the 64 state blocks held by the same index of wide as the observations. `owner`: a state block held by index w of wide belongs to one of the compartments w * 8 to w * 8 + 7.
All inputs are finite; a program needn't handle non-finite values.
Results may differ from the reference program's by a relative error of at most 0.0069.
Values may be sent and summed in bfloat16 or wider, within the bound.
No kernel may reach another device: no remote copies, remote signals or barrier semaphores. Data moves between devices by JAX's collectives and lax.ppermute only.
A program may use at most 64 MiB of HBM per device.

```python
import math
import jax
import jax.numpy as jnp
from jax import lax

M = 1024
CLASSES = 128
S_DEV = 8192
P_DEV = 2048
COMP_DEV = 8
ITERS = 4
S = 65536
P_SIZE = 16384
NBLK_ALL = 512
NOB = 128
COMP = 64
N_WIDE = 8


def draw_owner(key, part):
    key = jax.random.fold_in(key, 11)
    block_count = S_DEV // CLASSES
    positions = jnp.arange(NBLK_ALL, dtype=jnp.int32)
    base_comp = positions // block_count * COMP_DEV
    offsets = jax.random.randint(key, (NBLK_ALL,), 0, COMP_DEV, dtype=jnp.int32)
    offsets = jnp.where(positions == 0, 0, offsets)
    offsets = jnp.where(positions == NBLK_ALL - 1, COMP_DEV - 1, offsets)
    return (base_comp + offsets).astype(jnp.int32)


def plant(result, rng, low, largest):
    longest = result.shape.index(max(result.shape))
    spots = []
    for shift in (0, 1):
        where = [jax.random.randint(jax.random.fold_in(rng, axis), (), 0, length) for axis, length in enumerate(result.shape)]
        where[longest] = (where[longest] + shift) % result.shape[longest]
        spots.append(tuple(where))
    return result.at[spots[0]].set(low).at[spots[1]].set(largest)


def shard_levels(key, shape, cuts, smallest, top_value):
    def one(dim, parts):
        draws = jax.random.uniform(jax.random.fold_in(jax.random.fold_in(key, 6), dim), (parts,), jnp.float32, smallest / len(cuts), top_value / len(cuts))
        return jnp.repeat(jnp.exp(draws), shape[dim] // parts).reshape((-1,) + (1,) * (len(shape) - dim - 1))

    level = one(*cuts[0])
    for cut in cuts[1:]:
        level = level * one(*cut)
    return level


def centred(key, dims, deviation, reach, shards=(), held_as=jnp.bfloat16):
    array = jax.random.normal(key, dims, jnp.float32) * deviation
    if len(shards) > 0:
        array = shard_levels(key, dims, shards, -0.22, 0.18) * array
    return jnp.clip(array, min=-reach, max=reach).astype(held_as)


def setup_inputs(seed: int = 0) -> dict:
    key_list = jax.random.split(jax.random.key(seed), 7)
    ensemble = centred(key_list[0], (M, S), 1.0, 6.0, ((0, 4), (1, 8)))
    owner = draw_owner(jax.random.fold_in(key_list[6], 71), 0)
    inflation = jnp.clip(jax.random.uniform(key_list[2], (COMP,), jnp.float32, 1.0, 2.0), 1.0, 2.0)
    obs_block = plant(jax.random.randint(key_list[3], (NOB,), 0, S_DEV // CLASSES), jax.random.fold_in(key_list[3], 1), 0, (S_DEV // CLASSES) - 1).astype(jnp.int32)
    obs_value = centred(key_list[4], (P_SIZE,), 3.0, 12.0, ((0, 8),), jnp.float32)
    obs_std = jnp.clip(jnp.exp(math.log(300.0) - 5.7037825 * jax.random.uniform(key_list[5], (P_SIZE,), jnp.float32) ** shard_levels(key_list[5], (P_SIZE,), ((0, 8),), -0.2, 0.2)), 1.0, 300.0)
    return dict(ensemble=ensemble, owner=owner, inflation=inflation, obs_block=obs_block, obs_value=obs_value, obs_std=obs_std)


HIGH = lax.Precision.HIGHEST

def reference(ensemble, owner, inflation, obs_block, obs_value, obs_std):
    block_count = S_DEV // CLASSES
    obs_blocks = P_DEV // CLASSES
    scale_root = math.sqrt(M - 1)
    member_blocks = ensemble.reshape(M, N_WIDE, S_DEV).transpose(1, 0, 2)
    owner_ids = owner.reshape(N_WIDE, block_count)
    pick_rows = obs_block.reshape(N_WIDE, obs_blocks)
    obs_level = obs_value.reshape(N_WIDE, P_DEV)
    obs_sigma = obs_std.reshape(N_WIDE, P_DEV)

    def prepare(pieces):
        member_block, owner_part, pick_part, level_part, sigma_part = pieces
        state_mean = lax.optimization_barrier(jnp.sum(member_block, axis=0, dtype=jnp.float32)) / M
        row_factor = jnp.repeat(inflation[owner_part], CLASSES)
        anomaly = (row_factor * (member_block.astype(jnp.float32) - state_mean)).astype(jnp.bfloat16)
        observed = anomaly.reshape(M, block_count, CLASSES)[:, pick_part, :].reshape(M, P_DEV)
        observed_mean = state_mean.reshape(block_count, CLASSES)[pick_part].reshape(P_DEV)
        scaled = (observed.astype(jnp.float32) / (sigma_part * scale_root)).astype(jnp.bfloat16)
        innovation = (level_part - observed_mean) / sigma_part
        gram_part = jnp.dot(scaled, scaled.T, preferred_element_type=jnp.float32)
        projected_part = jnp.dot(scaled.astype(jnp.float32), innovation, precision=HIGH)
        return (state_mean, anomaly, gram_part, projected_part)
    means, anomalies, gram_parts, projected_parts = lax.map(prepare, (member_blocks, owner_ids, pick_rows, obs_level, obs_sigma))
    identity = jnp.eye(M, dtype=jnp.float32)
    gram_matrix = lax.optimization_barrier(jnp.sum(gram_parts, axis=0)) + identity
    projected = lax.optimization_barrier(jnp.sum(projected_parts, axis=0))
    frob_norm = jnp.sqrt(jnp.sum(gram_matrix * gram_matrix))
    unit_gram = gram_matrix / frob_norm
    iterate = identity
    for turn_index in range(ITERS):
        product_one = jnp.dot(unit_gram, iterate, precision=HIGH)
        product_two = jnp.dot(product_one, iterate, precision=HIGH)
        iterate = 1.5 * iterate - 0.5 * jnp.dot(product_two, iterate, precision=HIGH)
    root_matrix = iterate / jnp.sqrt(frob_norm)
    midway = jnp.dot(root_matrix, projected, precision=HIGH)
    mean_shift = jnp.dot(root_matrix, midway, precision=HIGH) / scale_root
    transform = (root_matrix + mean_shift[:, None]).astype(jnp.bfloat16)

    def apply_transform(pieces):
        state_mean, anomaly = pieces
        update = jnp.dot(transform.T, anomaly, preferred_element_type=jnp.float32)
        return (state_mean[None, :] + update).astype(jnp.bfloat16)
    outputs = lax.map(apply_transform, (means, anomalies))
    return outputs.transpose(1, 0, 2).reshape(M, S)
```

```python
import functools
import math

import jax
import jax.numpy as jnp
from jax import lax
from jax.experimental import pallas as pl
from jax.experimental.pallas import tpu as pltpu
from jax.sharding import PartitionSpec as P

CLASSES = 128
PAD = 16
LANES = 128
F32 = jnp.float32
BF16 = jnp.bfloat16
ANY = pl.BlockSpec(memory_space=pl.ANY)
HBM = pl.BlockSpec(memory_space=pltpu.HBM)
SMEM = pl.BlockSpec(memory_space=pltpu.SMEM)
VMEM = pl.BlockSpec(memory_space=pltpu.VMEM)
MIB = 1024 * 1024


def dot(a, b):
    return lax.dot_general(a, b, (((1,), (0,)), ((), ())), preferred_element_type=F32)


def dot_nt(a, b):
    return lax.dot_general(a, b, (((1,), (1,)), ((), ())), preferred_element_type=F32)


def swap(x, axis, mask):
    size = lax.axis_size(axis)
    return lax.ppermute(x, axis, [(i, i ^ mask) for i in range(size)])


def masks_of(size):
    return [1 << b for b in range(size.bit_length() - 1)]


def far(x):
    held = {0: x}
    for mask in reversed(masks_of(lax.axis_size("narrow"))[1:]):
        for m in list(held):
            held[m ^ mask] = swap(held[m], "narrow", mask)
    return held


def near(held, own=None):
    both = dict(held)
    for m in held:
        both[m ^ 1] = swap(held[m], "narrow", 1) if m or own is None else own
    return [both[m] for m in range(len(both))]


def tie(*trees):
    return lax.optimization_barrier(trees)


def lead_kernel(obs_ref, ens_ref, order_ref, lead_ref, mark_ref, sem):
    nob = obs_ref.shape[0]
    nblk = mark_ref.shape[0]

    for i in range(nblk):
        mark_ref[i] = 0
    place = 0
    for i in range(nob):
        block = obs_ref[i]
        order_ref[place] = block
        place = place + 1 - mark_ref[block]
        mark_ref[block] = 1
    for i in range(nblk):
        order_ref[place] = i
        place = place + 1 - mark_ref[i]
    copy_blocks(order_ref, 0, ens_ref, lead_ref, sem)
    wait_blocks(ens_ref, lead_ref, sem)


def copy_blocks(order_ref, first, ens_ref, out_ref, sem):
    count = out_ref.shape[1] // CLASSES

    def start(q, c):
        src = pl.multiple_of(order_ref[first + q] * CLASSES, CLASSES)
        dst = pl.multiple_of(q * CLASSES, CLASSES)
        pltpu.make_async_copy(
            ens_ref.at[:, pl.ds(src, CLASSES)], out_ref.at[:, pl.ds(dst, CLASSES)], sem
        ).start()
        return c

    lax.fori_loop(0, count, start, 0, unroll=4)


def wait_blocks(ens_ref, out_ref, sem):
    pltpu.make_async_copy(ens_ref.at[:, pl.ds(0, out_ref.shape[1])], out_ref, sem).wait()


def lead_blocks(obs_block, ensemble, lead):
    members, states = ensemble.shape
    nblk = states // CLASSES
    return pl.pallas_call(
        lead_kernel,
        out_shape=(
            jax.ShapeDtypeStruct((2 * nblk,), jnp.int32),
            jax.ShapeDtypeStruct((members, lead * CLASSES), BF16),
        ),
        in_specs=[SMEM, HBM],
        out_specs=(SMEM, VMEM),
        scratch_shapes=[pltpu.SMEM((nblk,), jnp.int32), pltpu.SemaphoreType.DMA],
        compiler_params=pltpu.CompilerParams(vmem_limit_bytes=60 * MIB),
        name="lead_blocks",
    )(obs_block, ensemble)


def rest_kernel(lead, order_ref, ens_ref, *refs):
    outs, sems = refs[:-1], refs[-1]
    first = lead
    for c, out in enumerate(outs):
        copy_blocks(order_ref, first, ens_ref, out, sems.at[c])
        first += out.shape[1] // CLASSES
    for c, out in enumerate(outs):
        wait_blocks(ens_ref, out, sems.at[c])


def rest_blocks(order, ensemble, lead, sizes):
    members = ensemble.shape[0]
    count = len(sizes)
    return pl.pallas_call(
        functools.partial(rest_kernel, lead),
        out_shape=[jax.ShapeDtypeStruct((members, n * CLASSES), BF16) for n in sizes],
        in_specs=[SMEM, HBM],
        out_specs=[VMEM] * count,
        scratch_shapes=[pltpu.SemaphoreType.DMA((count,))],
        compiler_params=pltpu.CompilerParams(vmem_limit_bytes=56 * MIB),
        name="rest_blocks",
    )(order, ensemble)


def split_rows(row, count, terms):
    ids = lax.broadcasted_iota(jnp.int32, (count, row.shape[1]), 0)
    out = jnp.zeros((count, row.shape[1]), F32)
    left = row
    for t in range(terms):
        part = left.astype(BF16).astype(F32)
        out = jnp.where(ids == t, part, out)
        left = left - part
    return out.astype(BF16)


def tail_of(rows, count):
    high = rows.astype(BF16).astype(F32)
    below = jnp.zeros((count - 2 * rows.shape[0], rows.shape[1]), F32)
    return jnp.concatenate([high, rows - high, below], axis=0).astype(BF16)


def rows_of_tail(tail):
    tail = tail.astype(F32)
    return tail[:8] + tail[8:16]


def slab_width(own, local):
    pairs = own * (own - 1) // 2 + own * own // 2
    return own * 3 // 2 * (local // 2) + pairs * local


def is_high(index_ref):
    return lax.rem(index_ref[0], 2) == 1


def gram_kernel(parts, scale_root, width, *refs):
    index_ref = refs[0]
    raws = refs[1 : parts + 1]
    factor_ref, weight_ref, root_ref, level_ref = refs[parts + 1 : parts + 5]
    keep_one, send_one, keep_two, send_two, halves, scaled, own, pulls = refs[parts + 5 :]
    local, cols = raws[0].shape
    half = local // 2
    count = parts // 2
    for first in range(0, cols, width):
        part = slice(first, first + width)
        factor = factor_ref[:, part]
        values = [r[:, part].astype(F32) for r in raws]
        total = jnp.sum(values[0], axis=0, keepdims=True)
        for v in values[1:]:
            total = total + jnp.sum(v, axis=0, keepdims=True)
        mean = total / (local * parts)
        both = factor * root_ref[:, part]
        for m, v in enumerate(values):
            v = v - mean
            place = (m % 2 * count + m // 2) * local
            scaled[place : place + local, part] = (both * v).astype(BF16)
            if m % 2 == 0:
                own[m // 2 * local : (m // 2 + 1) * local, part] = (factor * v).astype(BF16)
        pull = level_ref[:, part] - mean * weight_ref[:, part] * scale_root
        pulls[:, part] = split_rows(pull, PAD, 3)

    high = is_high(index_ref)
    at = [0, 0]

    def put(which, value):
        halves[which, :, at[which] : at[which] + value.shape[1]] = value.astype(BF16)
        at[which] += value.shape[1]

    side = count * local
    blocks = {}
    for j in range(count):
        product = dot_nt(scaled[j * local : side, :], scaled[j * local : (j + 1) * local, :])
        for i in range(j, count):
            blocks[i, j] = product[(i - j) * local : (i - j + 1) * local]
    for i in range(count):
        put(i % 2, blocks[i, i][:half, :half])
        put(1 - i % 2, blocks[i, i][half:, :])
    for i in range(count):
        for j in range(i):
            put(0, blocks[i, j][:half])
            put(1, blocks[i, j][half:])
    low = scaled[pl.ds(pl.multiple_of(jnp.where(high, side, 0), side), side), :]
    for c in range(count // 2):
        first = jnp.where(high, (c + count // 2) * local, side + c * local)
        product = dot_nt(low, scaled[pl.ds(pl.multiple_of(first, local), local), :])
        for i in range(count):
            blocks[i, c] = product[i * local : (i + 1) * local]
    for i in range(count):
        for c in range(count // 2):
            put(0, blocks[i, c][:half])
            put(1, blocks[i, c][half:])
    row = jnp.sum(dot_nt(pulls[...], own[...]), axis=0, keepdims=True)
    ids = lax.broadcasted_iota(jnp.int32, (8, LANES), 0)
    rows = jnp.zeros((8, LANES), F32)
    for r in range(side // LANES):
        rows = jnp.where(ids == r, row[:, r * LANES : (r + 1) * LANES], rows)
    quarter = half // 2
    across = halves.shape[2]
    mine = pl.multiple_of(index_ref[1] * quarter, quarter)
    other = pl.multiple_of((1 - index_ref[1]) * quarter, quarter)
    for ref, which, first in (
        (keep_one, 0, mine),
        (send_one, 0, other),
        (keep_two, 1, mine),
        (send_two, 1, other),
    ):
        ref[:, :across] = halves[which, pl.ds(first, quarter), :]
        if which == 0:
            ref[:, across:] = tail_of(rows, quarter)


def gram_rows(index, raws, factor, weight, root, level, scale_root, width=256):
    parts = len(raws)
    local, cols = raws[0].shape
    half = local // 2
    members = local * parts
    across = slab_width(parts // 2, local)
    return pl.pallas_call(
        functools.partial(gram_kernel, parts, scale_root, width),
        out_shape=(
            jax.ShapeDtypeStruct((half // 2, across + LANES), BF16),
            jax.ShapeDtypeStruct((half // 2, across + LANES), BF16),
            jax.ShapeDtypeStruct((half // 2, across), BF16),
            jax.ShapeDtypeStruct((half // 2, across), BF16),
        ),
        in_specs=[SMEM] + [VMEM] * (parts + 4),
        out_specs=(VMEM, VMEM, VMEM, VMEM),
        scratch_shapes=[
            pltpu.VMEM((2, half, across), BF16),
            pltpu.VMEM((members, cols), BF16),
            pltpu.VMEM((members // 2, cols), BF16),
            pltpu.VMEM((PAD, cols), BF16),
        ],
        compiler_params=pltpu.CompilerParams(vmem_limit_bytes=24 * MIB),
        cost_estimate=pl.CostEstimate(flops=1024, bytes_accessed=1024, transcendentals=0),
        name="gram_rows",
    )(index, *raws, factor, weight, root, level)


def add_kernel(across, a_ref, b_ref, out_ref):
    both = a_ref[:, :across].astype(F32) + b_ref[:, :across].astype(F32)
    out_ref[:, :across] = both.astype(BF16)
    if across < a_ref.shape[1]:
        rows = rows_of_tail(a_ref[:, across:]) + rows_of_tail(b_ref[:, across:])
        out_ref[:, across:] = tail_of(rows, a_ref.shape[0])


def add_slabs(a, b, across):
    return pl.pallas_call(
        functools.partial(add_kernel, across),
        out_shape=jax.ShapeDtypeStruct(a.shape, BF16),
        in_specs=[VMEM, VMEM],
        out_specs=VMEM,
        compiler_params=pltpu.CompilerParams(vmem_limit_bytes=16 * MIB),
        name="add_slabs",
    )(a, b)


def join_kernel(index_ref, one_ref, other_one_ref, two_ref, other_two_ref, out_ref):
    quarter, across = two_ref.shape
    mine = pl.multiple_of(index_ref[1] * quarter, quarter)
    other = pl.multiple_of((1 - index_ref[1]) * quarter, quarter)
    out_ref[pl.ds(mine, quarter), :across] = one_ref[:, :across]
    out_ref[pl.ds(other, quarter), :across] = other_one_ref[:, :across]
    out_ref[pl.ds(2 * quarter + mine, quarter), :across] = two_ref[...]
    out_ref[pl.ds(2 * quarter + other, quarter), :across] = other_two_ref[...]
    out_ref[:quarter, across:] = one_ref[:, across:]
    out_ref[quarter:, across:] = jnp.zeros((3 * quarter, out_ref.shape[1] - across), BF16)


def join_slabs(index, one, other_one, two, other_two):
    quarter = two.shape[0]
    return pl.pallas_call(
        join_kernel,
        out_shape=jax.ShapeDtypeStruct((4 * quarter, one.shape[1]), BF16),
        in_specs=[SMEM] + [VMEM] * 4,
        out_specs=VMEM,
        compiler_params=pltpu.CompilerParams(vmem_limit_bytes=16 * MIB),
        name="join_slabs",
    )(index, one, other_one, two, other_two)


def root_kernel(parts, scale_root, tile, *refs):
    index_ref, mine_ref, sibling_ref, out_ref = refs[:4]
    u, ub, rest, rb, work, wb, wb2, tail = refs[4:]
    members = u.shape[0]
    local = members // parts
    half = local // 2
    count = parts // 2
    diag = lax.broadcasted_iota(jnp.int32, (local, local), 0) == lax.broadcasted_iota(
        jnp.int32, (local, local), 1
    )
    square = jnp.zeros((1, members), F32)

    def span(m):
        return slice(m * local, (m + 1) * local)

    def put_pair(i, j, block):
        u[span(i), span(j)] = block
        u[span(j), span(i)] = block.T

    high = is_high(index_ref)
    crossed = []
    for side, slab in enumerate((mine_ref, sibling_ref)):
        at = [0, 0]

        def take(which, width):
            first = at[which]
            at[which] += width
            return slab[which * half : (which + 1) * half, first : first + width].astype(F32)

        for i in range(count):
            corner = take(i % 2, half)
            lower = take(1 - i % 2, local)
            upper = jnp.concatenate([corner, lower[:, :half].T], axis=1)
            block = jnp.concatenate([upper, lower], axis=0) + jnp.where(diag, 1.0, 0.0)
            u[span(2 * i + side), span(2 * i + side)] = block
        for i in range(count):
            for j in range(i):
                block = jnp.concatenate([take(0, local), take(1, local)], axis=0)
                put_pair(2 * i + side, 2 * j + side, block)
        for i in range(count):
            for c in range(count // 2):
                block = jnp.concatenate([take(0, local), take(1, local)], axis=0)
                crossed.append((side, i, c, block))
    for side, i, c, block in crossed:

        @pl.when(high)
        def _():
            put_pair(2 * i + 1, 2 * (c + (1 - side) * (count // 2)), block)

        @pl.when(jnp.logical_not(high))
        def _():
            put_pair(2 * i, 2 * (c + side * (count // 2)) + 1, block)

    for m in range(parts):
        part = u[m * local : (m + 1) * local, :]
        square = square + jnp.sum(part * part, axis=0, keepdims=True)
    frob = jnp.sqrt(jnp.sum(square, axis=1, keepdims=True))

    def each_column(body):
        for first in range(0, members, tile):
            body(slice(first, members), slice(first, first + tile))

    def mirror(ref, below, col, value):
        value = value.astype(BF16)
        ref[below, col] = value
        for first in range(col.stop, members, tile):
            block = value[first - col.start : first - col.start + tile]
            ref[col, first : first + tile] = block.T

    inverse = 1.0 / frob
    unit = u[...] * inverse
    u[...] = unit
    ub[:members, :] = unit.astype(BF16)

    def square_columns(below, col):
        v = dot(ub[below, :], ub[:members, col])
        unit = u[below, col]
        mirror(wb, below, col, v)
        mirror(wb2, below, col, 0.0625 * v - 0.5625 * unit)
        rest[below, col] = 1.6875 * v - 2.4375 * unit

    def second_columns(below, col):
        r = rest[below, col] + dot(wb[below, :], wb2[:, col])
        rest[below, col] = r
        mirror(rb, below, col, r)

    each_column(square_columns)
    each_column(second_columns)

    sums = []
    for slab in (mine_ref, sibling_ref):
        rows = rows_of_tail(slab[:PAD, slab.shape[1] - LANES :])
        pieces = [rows[r : r + 1, :] for r in range(count * local // LANES)]
        sums.append(jnp.concatenate(pieces, axis=1))
    projected = jnp.concatenate(
        [sums[m % 2][:, m // 2 * local : (m // 2 + 1) * local] for m in range(parts)], axis=1
    )
    ub[members:, :] = split_rows(projected, PAD, 2)

    def z_columns(below, col):
        y = dot(ub[below.start :, :], rb[:members, col])
        z = 2.25 * u[below, col] + y[:-PAD]
        tail[:, col] = y[-PAD:]
        work[below, col] = z
        mirror(wb, below, col, z)

    def a_columns(below, col):
        a = 2.25 * work[below, col] + dot(wb[below, :], rb[:members, col])
        mirror(wb2, below, col, a)
        rest[below, col] = 1.5 * rest[below, col] - 1.125 * a

    def third_columns(below, col):
        y = dot(rb[below.start :, :], wb2[:, col])
        r = rest[below, col] - 0.5 * y[:-PAD]
        tail[:, col] = y[-PAD:]
        rest[below, col] = r
        mirror(wb, below, col, r)

    each_column(z_columns)
    second_row = 2.25 * projected + jnp.sum(tail[...], axis=0, keepdims=True)
    rb[members:, :] = split_rows(second_row, PAD, 2)
    each_column(a_columns)
    each_column(third_columns)
    third_row = 1.5 * second_row - 0.5 * jnp.sum(tail[...], axis=0, keepdims=True)
    rest_rows = rest[:, :local].T

    def times(slab, row, mat):
        y = dot(jnp.concatenate([slab.astype(BF16), split_rows(row, PAD, 2)], axis=0), mat)
        return y[:local], jnp.sum(y[local:], axis=0, keepdims=True)

    def row_times(row, mat):
        return jnp.sum(dot(split_rows(row, PAD, 2), mat), axis=0, keepdims=True)

    unit_cols = ub[:members, :]
    rest_cols = wb[...]
    y, z_row = times(rest_rows, third_row, unit_cols)
    z = 3.375 * u[:local, :] + y
    y, a_row = times(z, z_row, rest_cols)
    a, a_row = 3.375 * z + y, 3.375 * z_row + a_row
    y, b_row = times(a, a_row, rest_cols)
    b, b_row = 3.375 * a + y, 3.375 * a_row + b_row
    eye = jnp.concatenate(
        [jnp.where(diag, 3.375, 0.0), jnp.zeros((local, members - local), F32)], axis=1
    )
    fourth = 1.5 * (eye + rest_rows) - 0.5 * b
    midway = 1.5 * third_row - 0.5 * b_row
    y_row = 3.375 * midway + row_times(midway, rest_cols)
    z_row = row_times(y_row, unit_cols)
    a_row = 3.375 * z_row + row_times(z_row, rest_cols)
    b_row = 3.375 * a_row + row_times(a_row, rest_cols)
    shift = (1.5 * y_row - 0.5 * b_row) * (inverse / scale_root)
    out_ref[...] = (fourth * jnp.sqrt(inverse) + shift).astype(BF16)


def transform_rows(index, mine, sibling, parts, scale_root, tile=256):
    local = mine.shape[0]
    members = local * parts
    wide = pltpu.VMEM((members, members), F32)
    narrow = pltpu.VMEM((members, members), BF16)
    longer = pltpu.VMEM((members + PAD, members), BF16)
    return pl.pallas_call(
        functools.partial(root_kernel, parts, scale_root, tile),
        out_shape=jax.ShapeDtypeStruct((local, members), BF16),
        in_specs=[SMEM] + [VMEM] * 2,
        out_specs=VMEM,
        scratch_shapes=[wide, longer, wide, longer, wide, narrow, narrow]
        + [pltpu.VMEM((PAD, members), F32)],
        compiler_params=pltpu.CompilerParams(vmem_limit_bytes=36 * MIB),
        cost_estimate=pl.CostEstimate(flops=1024, bytes_accessed=1024, transcendentals=0),
        name="transform_rows",
    )(index, mine, sibling)


def sums_kernel(width, *refs):
    out_ref = refs[-1]
    for first in range(0, out_ref.shape[1], width):
        part = slice(first, min(first + width, out_ref.shape[1]))
        out_ref[:, part] = column_sums([r[:, part] for r in refs[:-1]])


def column_sums(pieces):
    total = jnp.sum(pieces[0].astype(F32), axis=0, keepdims=True)
    for piece in pieces[1:]:
        total = total + jnp.sum(piece.astype(F32), axis=0, keepdims=True)
    return total


def sums(pieces, width=256):
    return pl.pallas_call(
        functools.partial(sums_kernel, width),
        out_shape=jax.ShapeDtypeStruct((1, pieces[0].shape[1]), F32),
        in_specs=[VMEM] * len(pieces),
        out_specs=VMEM,
        compiler_params=pltpu.CompilerParams(vmem_limit_bytes=16 * MIB),
        cost_estimate=pl.CostEstimate(flops=1024, bytes_accessed=1024, transcendentals=0),
        name="sums",
    )(*pieces)


def update_kernel(width, parts, start, summed, order_ref, t_ref, factor_ref, *refs):
    raws, totals = refs[: parts * len(summed)], refs[parts * len(summed) : (parts + 1) * len(summed)]
    out_ref, buf, sem = refs[-3:]
    local, members = t_ref.shape
    rows = jnp.sum(t_ref[...].astype(F32), axis=1, keepdims=True)
    col = 0
    for chunk, (done, total_ref) in enumerate(zip(summed, totals)):
        held = raws[chunk * parts : (chunk + 1) * parts]
        for first in range(0, held[0].shape[1], width):
            count = min(width, held[0].shape[1] - first)
            part = slice(first, first + count)
            pieces = [r[:, part] for r in held]
            total = total_ref[:, part]
            if done < parts:
                total = total + column_sums(pieces[done:])
            mean = total / members
            factor = factor_ref[:, start + col : start + col + count]
            product = dot(t_ref[...], jnp.concatenate(pieces, axis=0))
            buf[:, col : col + count] = (
                factor * product + (mean - (mean * factor) * rows)
            ).astype(BF16)
            for q in range(0, count, CLASSES):
                src = col + q
                dst = pl.multiple_of(order_ref[(start + src) // CLASSES] * CLASSES, CLASSES)
                pltpu.make_async_copy(
                    buf.at[:, pl.ds(src, CLASSES)], out_ref.at[:, pl.ds(dst, CLASSES)], sem
                ).start()
            col += count
    pltpu.make_async_copy(buf, out_ref.at[:, pl.ds(0, col)], sem).wait()


def update(order, transform, factor, chunks, totals, summed, start, result=None, width=512):
    local, members = transform.shape
    parts = len(chunks[0])
    states = factor.shape[1]
    cols = sum(raws[0].shape[1] for raws in chunks)
    raws = [x for held in chunks for x in held]
    extra = [] if result is None else [result]
    inputs = raws + totals
    return pl.pallas_call(
        functools.partial(update_kernel, width, parts, start, summed),
        out_shape=jax.ShapeDtypeStruct((local, states), BF16),
        in_specs=[SMEM, VMEM, VMEM] + [VMEM] * len(inputs) + [ANY] * len(extra),
        out_specs=ANY,
        scratch_shapes=[pltpu.VMEM((local, cols), BF16), pltpu.SemaphoreType.DMA],
        input_output_aliases={3 + len(inputs): 0} if extra else {},
        compiler_params=pltpu.CompilerParams(vmem_limit_bytes=24 * MIB),
        cost_estimate=pl.CostEstimate(flops=1024, bytes_accessed=1024, transcendentals=0),
        name="update",
    )(order, transform, factor, *inputs, *extra)


def on_device(ensemble, owner, inflation, obs_block, obs_value, obs_std):
    local, states = ensemble.shape
    parts = lax.axis_size("narrow")
    members = local * parts
    nblk = states // CLASSES
    nob = obs_block.shape[0]
    scale_root = math.sqrt(members - 1)

    order, lead = lead_blocks(obs_block, ensemble, nob)
    lead_far = far(lead)
    left = nblk - nob
    sizes = [left * 30 // 48]
    sizes.append(left - sum(sizes))
    starts = [nob * CLASSES]
    for n in sizes[:-1]:
        starts.append(starts[-1] + n * CLASSES)
    rest = list(rest_blocks(order, ensemble, nob, sizes))

    pick = order[:nblk, None] == jnp.arange(nblk, dtype=jnp.int32)[None, :]
    owner_new = jnp.sum(jnp.where(pick, owner[None, :], 0), axis=1)
    comps = jnp.arange(inflation.shape[0], dtype=jnp.int32)
    factor_new = jnp.sum(
        jnp.where(owner_new[:, None] == comps[None, :], inflation[None, :], 0.0), axis=1
    )
    factor = jnp.repeat(factor_new, CLASSES).reshape(1, states)
    match = (order[:nob, None] == obs_block[None, :])[:, :, None]
    inverse = 1.0 / (obs_std * obs_std)
    weight = jnp.sum(jnp.where(match, inverse.reshape(1, nob, CLASSES), 0.0), axis=1)
    weight = weight.reshape(1, nob * CLASSES) / (members - 1)
    level = jnp.sum(jnp.where(match, (obs_value * inverse).reshape(1, nob, CLASSES), 0.0), axis=1)
    level = level.reshape(1, nob * CLASSES) / scale_root

    root = jnp.sqrt(weight)
    index = jnp.stack([lax.axis_index("narrow"), lax.rem(lax.axis_index("wide"), 2)])
    fars = [far(chunk) for chunk in rest]
    owns = [swap(chunk, "narrow", 1) for chunk in rest]
    lead_far, lead_own, rest, factor, weight, root, level = tie(
        lead_far, swap(lead, "narrow", 1), rest, factor, weight, root, level
    )
    lead_all = near(lead_far, lead_own)
    one, send_one, two, send_two = gram_rows(
        index, lead_all, factor, weight, root, level, scale_root
    )

    across = two.shape[1]
    masks = masks_of(lax.axis_size("wide"))
    steps = masks + [1]
    for slot in range(len(steps) + 1):
        one, two, send_one, send_two = tie(one, two, send_one, send_two)
        got = []
        if slot < len(steps):
            got.append(swap(send_one if slot == 0 else one, "wide", steps[slot]))
        if slot > 0:
            got.append(swap(send_two if slot == 1 else two, "wide", steps[slot - 1]))
        if slot == 0:
            total = sums(lead_all)
            got, total = tie(got, total)
        elif slot == 1:
            early = [sums([chunk, own]) for chunk, own in zip(rest, owns)]
            got, early, owns = tie(got, early, owns)
        elif slot == len(steps) - 1:
            got, fars[0] = tie(got, fars[0])
        else:
            (got,) = tie(got)
        if slot < len(masks):
            one = add_slabs(one, got[0], across)
        elif slot == len(masks):
            other_one = got[0]
        if 0 < slot <= len(masks):
            two = add_slabs(two, got[-1], across)
        elif slot > len(masks):
            other_two = got[-1]
    slab = join_slabs(index, one, other_one, two, other_two)
    sibling, all_one = tie(swap(slab, "narrow", 1), near(fars[0], owns[0]))
    transform = transform_rows(index, slab, sibling, parts, scale_root)
    result = update(order, transform, factor, [all_one], [early[0]], [2], starts[0])
    fars[1], result = tie(fars[1], result)
    all_two = near(fars[1], owns[1])
    result = update(order, transform, factor, [lead_all], [total], [parts], 0, result)
    return update(order, transform, factor, [all_two], [early[1]], [2], starts[1], result)


def solution(mesh):
    return jax.shard_map(
        on_device,
        mesh=mesh,
        in_specs=(P("narrow", "wide"), P("wide"), P(), P("wide"), P("wide"), P("wide")),
        out_specs=P("narrow", "wide"),
        check_vma=False,
    )
```

```python
import functools
import math

import jax
import jax.numpy as jnp
from jax import lax
from jax.experimental import pallas as pl
from jax.experimental.pallas import tpu as pltpu
from jax.sharding import PartitionSpec as P

CLASSES = 128
PAD = 16
LANES = 128
F32 = jnp.float32
BF16 = jnp.bfloat16
ANY = pl.BlockSpec(memory_space=pl.ANY)
HBM = pl.BlockSpec(memory_space=pltpu.HBM)
SMEM = pl.BlockSpec(memory_space=pltpu.SMEM)
VMEM = pl.BlockSpec(memory_space=pltpu.VMEM)
MIB = 1024 * 1024


def dot(a, b):
    return lax.dot_general(a, b, (((1,), (0,)), ((), ())), preferred_element_type=F32)


def dot_nt(a, b):
    return lax.dot_general(a, b, (((1,), (1,)), ((), ())), preferred_element_type=F32)


def swap(x, axis, mask):
    size = lax.axis_size(axis)
    return lax.ppermute(x, axis, [(i, i ^ mask) for i in range(size)])


def masks_of(size):
    return [1 << b for b in range(size.bit_length() - 1)]


def far(x):
    held = {0: x}
    for mask in reversed(masks_of(lax.axis_size("narrow"))[1:]):
        for m in list(held):
            held[m ^ mask] = swap(held[m], "narrow", mask)
    return held


def near(held, own=None):
    both = dict(held)
    for m in held:
        both[m ^ 1] = swap(held[m], "narrow", 1) if m or own is None else own
    return [both[m] for m in range(len(both))]


def tie(*trees):
    return lax.optimization_barrier(trees)


def lead_kernel(obs_ref, ens_ref, order_ref, lead_ref, mark_ref, sem):
    nob = obs_ref.shape[0]
    nblk = mark_ref.shape[0]

    for i in range(nblk):
        mark_ref[i] = 0
    place = 0
    for i in range(nob):
        block = obs_ref[i]
        order_ref[place] = block
        place = place + 1 - mark_ref[block]
        mark_ref[block] = 1
    for i in range(nblk):
        order_ref[place] = i
        place = place + 1 - mark_ref[i]
    copy_blocks(order_ref, 0, ens_ref, lead_ref, sem)
    wait_blocks(ens_ref, lead_ref, sem)


def copy_blocks(order_ref, first, ens_ref, out_ref, sem):
    count = out_ref.shape[1] // CLASSES

    def start(q, c):
        src = pl.multiple_of(order_ref[first + q] * CLASSES, CLASSES)
        dst = pl.multiple_of(q * CLASSES, CLASSES)
        pltpu.make_async_copy(
            ens_ref.at[:, pl.ds(src, CLASSES)], out_ref.at[:, pl.ds(dst, CLASSES)], sem
        ).start()
        return c

    lax.fori_loop(0, count, start, 0, unroll=4)


def wait_blocks(ens_ref, out_ref, sem):
    pltpu.make_async_copy(ens_ref.at[:, pl.ds(0, out_ref.shape[1])], out_ref, sem).wait()


def lead_blocks(obs_block, ensemble, lead):
    members, states = ensemble.shape
    nblk = states // CLASSES
    return pl.pallas_call(
        lead_kernel,
        out_shape=(
            jax.ShapeDtypeStruct((2 * nblk,), jnp.int32),
            jax.ShapeDtypeStruct((members, lead * CLASSES), BF16),
        ),
        in_specs=[SMEM, HBM],
        out_specs=(SMEM, VMEM),
        scratch_shapes=[pltpu.SMEM((nblk,), jnp.int32), pltpu.SemaphoreType.DMA],
        compiler_params=pltpu.CompilerParams(vmem_limit_bytes=60 * MIB),
        name="lead_blocks",
    )(obs_block, ensemble)


def rest_kernel(lead, order_ref, ens_ref, *refs):
    outs, sems = refs[:-1], refs[-1]
    first = lead
    for c, out in enumerate(outs):
        copy_blocks(order_ref, first, ens_ref, out, sems.at[c])
        first += out.shape[1] // CLASSES
    for c, out in enumerate(outs):
        wait_blocks(ens_ref, out, sems.at[c])


def rest_blocks(order, ensemble, lead, sizes):
    members = ensemble.shape[0]
    count = len(sizes)
    return pl.pallas_call(
        functools.partial(rest_kernel, lead),
        out_shape=[jax.ShapeDtypeStruct((members, n * CLASSES), BF16) for n in sizes],
        in_specs=[SMEM, HBM],
        out_specs=[VMEM] * count,
        scratch_shapes=[pltpu.SemaphoreType.DMA((count,))],
        compiler_params=pltpu.CompilerParams(vmem_limit_bytes=56 * MIB),
        name="rest_blocks",
    )(order, ensemble)


def split_rows(row, count, terms):
    ids = lax.broadcasted_iota(jnp.int32, (count, row.shape[1]), 0)
    out = jnp.zeros((count, row.shape[1]), F32)
    left = row
    for t in range(terms):
        part = left.astype(BF16).astype(F32)
        out = jnp.where(ids == t, part, out)
        left = left - part
    return out.astype(BF16)


def tail_of(rows, count):
    high = rows.astype(BF16).astype(F32)
    below = jnp.zeros((count - 2 * rows.shape[0], rows.shape[1]), F32)
    return jnp.concatenate([high, rows - high, below], axis=0).astype(BF16)


def rows_of_tail(tail):
    tail = tail.astype(F32)
    return tail[:8] + tail[8:16]


def slab_width(own, local):
    pairs = own * (own - 1) // 2 + own * own // 2
    return own * 3 // 2 * (local // 2) + pairs * local


def is_high(index_ref):
    return lax.rem(index_ref[0], 2) == 1


def gram_kernel(parts, scale_root, width, *refs):
    index_ref = refs[0]
    raws = refs[1 : parts + 1]
    factor_ref, weight_ref, root_ref, level_ref = refs[parts + 1 : parts + 5]
    keep_one, send_one, keep_two, send_two, halves, scaled, own, pulls = refs[parts + 5 :]
    local, cols = raws[0].shape
    half = local // 2
    count = parts // 2
    for first in range(0, cols, width):
        part = slice(first, first + width)
        factor = factor_ref[:, part]
        mean = column_sums([r[:, part] for r in raws]) / (local * parts)
        both = factor * root_ref[:, part]
        for m, r in enumerate(raws):
            v = r[:, part].astype(F32) - mean
            place = (m % 2 * count + m // 2) * local
            scaled[place : place + local, part] = (both * v).astype(BF16)
            if m % 2 == 0:
                own[m // 2 * local : (m // 2 + 1) * local, part] = (factor * v).astype(BF16)
        pull = level_ref[:, part] - mean * weight_ref[:, part] * scale_root
        pulls[:, part] = split_rows(pull, PAD, 3)

    high = is_high(index_ref)
    at = [0, 0]

    def put(which, value):
        halves[which, :, at[which] : at[which] + value.shape[1]] = value.astype(BF16)
        at[which] += value.shape[1]

    side = count * local
    blocks = {}
    for j in range(count):
        product = dot_nt(scaled[j * local : side, :], scaled[j * local : (j + 1) * local, :])
        for i in range(j, count):
            blocks[i, j] = product[(i - j) * local : (i - j + 1) * local]
    for i in range(count):
        put(i % 2, blocks[i, i][:half, :half])
        put(1 - i % 2, blocks[i, i][half:, :])
    for i in range(count):
        for j in range(i):
            put(0, blocks[i, j][:half])
            put(1, blocks[i, j][half:])
    low = scaled[pl.ds(pl.multiple_of(jnp.where(high, side, 0), side), side), :]
    for c in range(count // 2):
        first = jnp.where(high, (c + count // 2) * local, side + c * local)
        product = dot_nt(low, scaled[pl.ds(pl.multiple_of(first, local), local), :])
        for i in range(count):
            blocks[i, c] = product[i * local : (i + 1) * local]
    for i in range(count):
        for c in range(count // 2):
            put(0, blocks[i, c][:half])
            put(1, blocks[i, c][half:])
    row = jnp.sum(dot_nt(pulls[...], own[...]), axis=0, keepdims=True)
    ids = lax.broadcasted_iota(jnp.int32, (8, LANES), 0)
    rows = jnp.zeros((8, LANES), F32)
    for r in range(side // LANES):
        rows = jnp.where(ids == r, row[:, r * LANES : (r + 1) * LANES], rows)
    quarter = half // 2
    across = halves.shape[2]
    mine = pl.multiple_of(index_ref[1] * quarter, quarter)
    other = pl.multiple_of((1 - index_ref[1]) * quarter, quarter)
    for ref, which, first in (
        (keep_one, 0, mine),
        (send_one, 0, other),
        (keep_two, 1, mine),
        (send_two, 1, other),
    ):
        ref[:, :across] = halves[which, pl.ds(first, quarter), :]
        if which == 0:
            ref[:, across:] = tail_of(rows, quarter)


def gram_rows(index, raws, factor, weight, root, level, scale_root, width=256):
    parts = len(raws)
    local, cols = raws[0].shape
    half = local // 2
    members = local * parts
    across = slab_width(parts // 2, local)
    return pl.pallas_call(
        functools.partial(gram_kernel, parts, scale_root, width),
        out_shape=(
            jax.ShapeDtypeStruct((half // 2, across + LANES), BF16),
            jax.ShapeDtypeStruct((half // 2, across + LANES), BF16),
            jax.ShapeDtypeStruct((half // 2, across), BF16),
            jax.ShapeDtypeStruct((half // 2, across), BF16),
        ),
        in_specs=[SMEM] + [VMEM] * (parts + 4),
        out_specs=(VMEM, VMEM, VMEM, VMEM),
        scratch_shapes=[
            pltpu.VMEM((2, half, across), BF16),
            pltpu.VMEM((members, cols), BF16),
            pltpu.VMEM((members // 2, cols), BF16),
            pltpu.VMEM((PAD, cols), BF16),
        ],
        compiler_params=pltpu.CompilerParams(vmem_limit_bytes=24 * MIB),
        cost_estimate=pl.CostEstimate(flops=1024, bytes_accessed=1024, transcendentals=0),
        name="gram_rows",
    )(index, *raws, factor, weight, root, level)


def add_kernel(across, a_ref, b_ref, out_ref):
    both = a_ref[:, :across].astype(F32) + b_ref[:, :across].astype(F32)
    out_ref[:, :across] = both.astype(BF16)
    if across < a_ref.shape[1]:
        rows = rows_of_tail(a_ref[:, across:]) + rows_of_tail(b_ref[:, across:])
        out_ref[:, across:] = tail_of(rows, a_ref.shape[0])


def add_slabs(a, b, across):
    return pl.pallas_call(
        functools.partial(add_kernel, across),
        out_shape=jax.ShapeDtypeStruct(a.shape, BF16),
        in_specs=[VMEM, VMEM],
        out_specs=VMEM,
        compiler_params=pltpu.CompilerParams(vmem_limit_bytes=16 * MIB),
        name="add_slabs",
    )(a, b)


def join_kernel(index_ref, one_ref, other_one_ref, two_ref, other_two_ref, out_ref):
    quarter, across = two_ref.shape
    mine = pl.multiple_of(index_ref[1] * quarter, quarter)
    other = pl.multiple_of((1 - index_ref[1]) * quarter, quarter)
    out_ref[pl.ds(mine, quarter), :across] = one_ref[:, :across]
    out_ref[pl.ds(other, quarter), :across] = other_one_ref[:, :across]
    out_ref[pl.ds(2 * quarter + mine, quarter), :across] = two_ref[...]
    out_ref[pl.ds(2 * quarter + other, quarter), :across] = other_two_ref[...]
    out_ref[:quarter, across:] = one_ref[:, across:]
    out_ref[quarter:, across:] = jnp.zeros((3 * quarter, out_ref.shape[1] - across), BF16)


def join_slabs(index, one, other_one, two, other_two):
    quarter = two.shape[0]
    return pl.pallas_call(
        join_kernel,
        out_shape=jax.ShapeDtypeStruct((4 * quarter, one.shape[1]), BF16),
        in_specs=[SMEM] + [VMEM] * 4,
        out_specs=VMEM,
        compiler_params=pltpu.CompilerParams(vmem_limit_bytes=16 * MIB),
        name="join_slabs",
    )(index, one, other_one, two, other_two)


def root_kernel(parts, scale_root, tile, *refs):
    index_ref, mine_ref, sibling_ref, out_ref, sums_ref = refs[:5]
    u, ub, rest, rb, wb, wb2, tail = refs[5:]
    members = u.shape[0]
    local = members // parts
    half = local // 2
    count = parts // 2
    diag = lax.broadcasted_iota(jnp.int32, (local, local), 0) == lax.broadcasted_iota(
        jnp.int32, (local, local), 1
    )
    square = jnp.zeros((1, members), F32)

    def span(m):
        return slice(m * local, (m + 1) * local)

    def put_pair(i, j, block):
        u[span(i), span(j)] = block
        u[span(j), span(i)] = block.T

    high = is_high(index_ref)
    crossed = []
    for side, slab in enumerate((mine_ref, sibling_ref)):
        at = [0, 0]

        def take(which, width):
            first = at[which]
            at[which] += width
            return slab[which * half : (which + 1) * half, first : first + width].astype(F32)

        for i in range(count):
            corner = take(i % 2, half)
            lower = take(1 - i % 2, local)
            upper = jnp.concatenate([corner, lower[:, :half].T], axis=1)
            block = jnp.concatenate([upper, lower], axis=0) + jnp.where(diag, 1.0, 0.0)
            u[span(2 * i + side), span(2 * i + side)] = block
        for i in range(count):
            for j in range(i):
                block = jnp.concatenate([take(0, local), take(1, local)], axis=0)
                put_pair(2 * i + side, 2 * j + side, block)
        for i in range(count):
            for c in range(count // 2):
                block = jnp.concatenate([take(0, local), take(1, local)], axis=0)
                crossed.append((side, i, c, block))
    for side, i, c, block in crossed:

        @pl.when(high)
        def _():
            put_pair(2 * i + 1, 2 * (c + (1 - side) * (count // 2)), block)

        @pl.when(jnp.logical_not(high))
        def _():
            put_pair(2 * i, 2 * (c + side * (count // 2)) + 1, block)

    for m in range(parts):
        part = u[m * local : (m + 1) * local, :]
        square = square + jnp.sum(part * part, axis=0, keepdims=True)
    frob = jnp.sqrt(jnp.sum(square, axis=1, keepdims=True))

    def each_column(body):
        for first in range(0, members, tile):
            body(slice(first, members), slice(first, first + tile))

    def mirror(ref, below, col, value):
        value = value.astype(BF16)
        ref[below, col] = value
        for first in range(col.stop, members, tile):
            block = value[first - col.start : first - col.start + tile]
            ref[col, first : first + tile] = block.T

    inverse = 1.0 / frob
    ub[:members, :] = (u[...] * inverse).astype(BF16)

    def square_columns(below, col):
        v = dot(ub[below, :], ub[:members, col])
        unit = u[below, col] * inverse
        mirror(wb, below, col, v)
        mirror(wb2, below, col, 0.0625 * v - 0.5625 * unit)
        rest[below, col] = 1.6875 * v - 2.4375 * unit

    def second_columns(below, col):
        r = rest[below, col] + dot(wb[below, :], wb2[:, col])
        rest[below, col] = r
        mirror(rb, below, col, r)

    each_column(square_columns)
    each_column(second_columns)

    sums = []
    for slab in (mine_ref, sibling_ref):
        rows = rows_of_tail(slab[:PAD, slab.shape[1] - LANES :])
        pieces = [rows[r : r + 1, :] for r in range(count * local // LANES)]
        sums.append(jnp.concatenate(pieces, axis=1))
    projected = jnp.concatenate(
        [sums[m % 2][:, m // 2 * local : (m // 2 + 1) * local] for m in range(parts)], axis=1
    )
    ub[members:, :] = split_rows(projected, PAD, 2)

    def z_columns(below, col):
        y = dot(ub[below.start :, :], rb[:members, col])
        z = (2.25 * inverse) * u[below, col] + y[:-PAD]
        tail[:, col] = y[-PAD:]
        mirror(wb, below, col, z)

    def a_columns(below, col):
        a = 2.25 * wb[below, col].astype(F32) + dot(wb[below, :], rb[:members, col])
        mirror(wb2, below, col, a)
        rest[below, col] = 1.5 * rest[below, col] - 1.125 * a

    def third_columns(below, col):
        y = dot(rb[below.start :, :], wb2[:, col])
        r = rest[below, col] - 0.5 * y[:-PAD]
        tail[:, col] = y[-PAD:]
        rest[below, col] = r
        mirror(wb, below, col, r)

    each_column(z_columns)
    second_row = 2.25 * projected + jnp.sum(tail[...], axis=0, keepdims=True)
    rb[members:, :] = split_rows(second_row, PAD, 2)
    each_column(a_columns)
    each_column(third_columns)
    third_row = 1.5 * second_row - 0.5 * jnp.sum(tail[...], axis=0, keepdims=True)
    rest_rows = rest[:, :local].T

    def times(slab, row, mat):
        y = dot(jnp.concatenate([slab.astype(BF16), split_rows(row, PAD, 2)], axis=0), mat)
        return y[:local], jnp.sum(y[local:], axis=0, keepdims=True)

    def row_times(row, mat):
        return jnp.sum(dot(split_rows(row, PAD, 2), mat), axis=0, keepdims=True)

    unit_cols = ub[:members, :]
    rest_cols = wb[...]
    y, z_row = times(rest_rows, third_row, unit_cols)
    z = (3.375 * inverse) * u[:local, :] + y
    y, a_row = times(z, z_row, rest_cols)
    a, a_row = 3.375 * z + y, 3.375 * z_row + a_row
    y, b_row = times(a, a_row, rest_cols)
    b, b_row = 3.375 * a + y, 3.375 * a_row + b_row
    eye = jnp.concatenate(
        [jnp.where(diag, 3.375, 0.0), jnp.zeros((local, members - local), F32)], axis=1
    )
    fourth = 1.5 * (eye + rest_rows) - 0.5 * b
    midway = 1.5 * third_row - 0.5 * b_row
    y_row = 3.375 * midway + row_times(midway, rest_cols)
    z_row = row_times(y_row, unit_cols)
    a_row = 3.375 * z_row + row_times(z_row, rest_cols)
    b_row = 3.375 * a_row + row_times(a_row, rest_cols)
    shift = (1.5 * y_row - 0.5 * b_row) * (inverse / scale_root)
    transform = (fourth * jnp.sqrt(inverse) + shift).astype(BF16)
    out_ref[...] = transform
    row_sums = jnp.sum(transform.astype(F32), axis=1, keepdims=True)
    sums_ref[...] = jnp.broadcast_to(row_sums, sums_ref.shape)


def transform_rows(index, mine, sibling, parts, scale_root, tile=256):
    local = mine.shape[0]
    members = local * parts
    wide = pltpu.VMEM((members, members), F32)
    narrow = pltpu.VMEM((members, members), BF16)
    longer = pltpu.VMEM((members + PAD, members), BF16)
    return pl.pallas_call(
        functools.partial(root_kernel, parts, scale_root, tile),
        out_shape=(
            jax.ShapeDtypeStruct((local, members), BF16),
            jax.ShapeDtypeStruct((local, LANES), F32),
        ),
        in_specs=[SMEM] + [VMEM] * 2,
        out_specs=(VMEM, VMEM),
        scratch_shapes=[wide, longer, wide, longer, narrow, narrow]
        + [pltpu.VMEM((PAD, members), F32)],
        compiler_params=pltpu.CompilerParams(vmem_limit_bytes=36 * MIB),
        cost_estimate=pl.CostEstimate(flops=1024, bytes_accessed=1024, transcendentals=0),
        name="transform_rows",
    )(index, mine, sibling)


def sums_kernel(width, *refs):
    out_ref = refs[-1]
    for first in range(0, out_ref.shape[1], width):
        part = slice(first, min(first + width, out_ref.shape[1]))
        out_ref[:, part] = column_sums([r[:, part] for r in refs[:-1]])


def column_sums(pieces):
    total = jnp.sum(pieces[0].astype(F32), axis=0, keepdims=True)
    for piece in pieces[1:]:
        total = total + jnp.sum(piece.astype(F32), axis=0, keepdims=True)
    return total


def sums(pieces, width=256):
    return pl.pallas_call(
        functools.partial(sums_kernel, width),
        out_shape=jax.ShapeDtypeStruct((1, pieces[0].shape[1]), F32),
        in_specs=[VMEM] * len(pieces),
        out_specs=VMEM,
        compiler_params=pltpu.CompilerParams(vmem_limit_bytes=16 * MIB),
        cost_estimate=pl.CostEstimate(flops=1024, bytes_accessed=1024, transcendentals=0),
        name="sums",
    )(*pieces)


def update_kernel(width, parts, start, summed, order_ref, t_ref, rows_ref, factor_ref, *refs):
    raws, totals = refs[: parts * len(summed)], refs[parts * len(summed) : (parts + 1) * len(summed)]
    out_ref, buf, sem = refs[-3:]
    local, members = t_ref.shape
    rows = rows_ref[:, :1]
    col = 0
    for chunk, (done, total_ref) in enumerate(zip(summed, totals)):
        held = raws[chunk * parts : (chunk + 1) * parts]
        for first in range(0, held[0].shape[1], width):
            count = min(width, held[0].shape[1] - first)
            part = slice(first, first + count)
            pieces = [r[:, part] for r in held]
            total = total_ref[:, part]
            if done < parts:
                total = total + column_sums(pieces[done:])
            mean = total / members
            factor = factor_ref[:, start + col : start + col + count]
            product = dot(t_ref[:, :local], held[0][:, part])
            for m in range(1, parts):
                product += dot(t_ref[:, m * local : (m + 1) * local], held[m][:, part])
            buf[:, col : col + count] = (
                factor * product + (mean - (mean * factor) * rows)
            ).astype(BF16)
            for q in range(0, count, CLASSES):
                src = col + q
                dst = pl.multiple_of(order_ref[(start + src) // CLASSES] * CLASSES, CLASSES)
                pltpu.make_async_copy(
                    buf.at[:, pl.ds(src, CLASSES)], out_ref.at[:, pl.ds(dst, CLASSES)], sem
                ).start()
            col += count
    pltpu.make_async_copy(buf, out_ref.at[:, pl.ds(0, col)], sem).wait()


def update(order, transform, factor, chunks, totals, summed, start, result=None, width=1024):
    local = transform[0].shape[0]
    parts = len(chunks[0])
    states = factor.shape[1]
    cols = sum(raws[0].shape[1] for raws in chunks)
    raws = [x for held in chunks for x in held]
    extra = [] if result is None else [result]
    inputs = raws + totals
    return pl.pallas_call(
        functools.partial(update_kernel, width, parts, start, summed),
        out_shape=jax.ShapeDtypeStruct((local, states), BF16),
        in_specs=[SMEM, VMEM, VMEM, VMEM] + [VMEM] * len(inputs) + [ANY] * len(extra),
        out_specs=ANY,
        scratch_shapes=[pltpu.VMEM((local, cols), BF16), pltpu.SemaphoreType.DMA],
        input_output_aliases={4 + len(inputs): 0} if extra else {},
        compiler_params=pltpu.CompilerParams(vmem_limit_bytes=24 * MIB),
        cost_estimate=pl.CostEstimate(flops=1024, bytes_accessed=1024, transcendentals=0),
        name="update",
    )(order, *transform, factor, *inputs, *extra)


def on_device(ensemble, owner, inflation, obs_block, obs_value, obs_std):
    local, states = ensemble.shape
    parts = lax.axis_size("narrow")
    members = local * parts
    nblk = states // CLASSES
    nob = obs_block.shape[0]
    scale_root = math.sqrt(members - 1)

    order, lead = lead_blocks(obs_block, ensemble, nob)
    lead_far = far(lead)
    left = nblk - nob
    sizes = [left * 33 // 48]
    sizes.append(left - sum(sizes))
    starts = [nob * CLASSES]
    for n in sizes[:-1]:
        starts.append(starts[-1] + n * CLASSES)
    rest = list(rest_blocks(order, ensemble, nob, sizes))

    pick = order[:nblk, None] == jnp.arange(nblk, dtype=jnp.int32)[None, :]
    owner_new = jnp.sum(jnp.where(pick, owner[None, :], 0), axis=1)
    comps = jnp.arange(inflation.shape[0], dtype=jnp.int32)
    factor_new = jnp.sum(
        jnp.where(owner_new[:, None] == comps[None, :], inflation[None, :], 0.0), axis=1
    )
    factor = jnp.repeat(factor_new, CLASSES).reshape(1, states)
    match = (order[:nob, None] == obs_block[None, :])[:, :, None]
    inverse = 1.0 / (obs_std * obs_std)
    weight = jnp.sum(jnp.where(match, inverse.reshape(1, nob, CLASSES), 0.0), axis=1)
    weight = weight.reshape(1, nob * CLASSES) / (members - 1)
    level = jnp.sum(jnp.where(match, (obs_value * inverse).reshape(1, nob, CLASSES), 0.0), axis=1)
    level = level.reshape(1, nob * CLASSES) / scale_root

    root = jnp.sqrt(weight)
    index = jnp.stack([lax.axis_index("narrow"), lax.rem(lax.axis_index("wide"), 2)])
    fars = [far(chunk) for chunk in rest]
    owns = [swap(chunk, "narrow", 1) for chunk in rest]
    lead_far, lead_own, rest, factor, weight, root, level = tie(
        lead_far, swap(lead, "narrow", 1), rest, factor, weight, root, level
    )
    lead_all = near(lead_far, lead_own)
    one, send_one, two, send_two = gram_rows(
        index, lead_all, factor, weight, root, level, scale_root
    )

    across = two.shape[1]
    masks = masks_of(lax.axis_size("wide"))
    steps = masks + [1]
    for slot in range(len(steps) + 1):
        one, two, send_one, send_two = tie(one, two, send_one, send_two)
        got = []
        if slot < len(steps):
            got.append(swap(send_one if slot == 0 else one, "wide", steps[slot]))
        if slot > 0:
            got.append(swap(send_two if slot == 1 else two, "wide", steps[slot - 1]))
        if slot == 0:
            total = sums(lead_all)
            got, total = tie(got, total)
        elif slot == 1:
            early = [sums([chunk, own]) for chunk, own in zip(rest, owns)]
            got, early, owns = tie(got, early, owns)
        elif slot == len(steps):
            got, fars[0] = tie(got, fars[0])
        else:
            (got,) = tie(got)
        if slot < len(masks):
            one = add_slabs(one, got[0], across)
        elif slot == len(masks):
            other_one = got[0]
        if 0 < slot <= len(masks):
            two = add_slabs(two, got[-1], across)
        elif slot > len(masks):
            other_two = got[-1]
    slab = join_slabs(index, one, other_one, two, other_two)
    sibling, all_one = tie(swap(slab, "narrow", 1), near(fars[0], owns[0]))
    transform = transform_rows(index, slab, sibling, parts, scale_root)
    result = update(order, transform, factor, [all_one], [early[0]], [2], starts[0])
    fars[1], result = tie(fars[1], result)
    all_two = near(fars[1], owns[1])
    result = update(order, transform, factor, [lead_all], [total], [parts], 0, result)
    return update(order, transform, factor, [all_two], [early[1]], [2], starts[1], result)


def solution(mesh):
    return jax.shard_map(
        on_device,
        mesh=mesh,
        in_specs=(P("narrow", "wide"), P("wide"), P(), P("wide"), P("wide"), P("wide")),
        out_specs=P("narrow", "wide"),
        check_vma=False,
    )
```

```python
import functools
import math

import jax
import jax.numpy as jnp
from jax import lax
from jax.experimental import pallas as pl
from jax.experimental.pallas import tpu as pltpu
from jax.sharding import PartitionSpec as P

CLASSES = 128
PAD = 16
LANES = 128
F32 = jnp.float32
BF16 = jnp.bfloat16
ANY = pl.BlockSpec(memory_space=pl.ANY)
HBM = pl.BlockSpec(memory_space=pltpu.HBM)
SMEM = pl.BlockSpec(memory_space=pltpu.SMEM)
VMEM = pl.BlockSpec(memory_space=pltpu.VMEM)
MIB = 1024 * 1024


def dot(a, b):
    return lax.dot_general(a, b, (((1,), (0,)), ((), ())), preferred_element_type=F32)


def dot_nt(a, b):
    return lax.dot_general(a, b, (((1,), (1,)), ((), ())), preferred_element_type=F32)


def swap(x, axis, mask):
    size = lax.axis_size(axis)
    return lax.ppermute(x, axis, [(i, i ^ mask) for i in range(size)])


def masks_of(size):
    return [1 << b for b in range(size.bit_length() - 1)]


def far(x):
    held = {0: x}
    for mask in reversed(masks_of(lax.axis_size("narrow"))[1:]):
        for m in list(held):
            held[m ^ mask] = swap(held[m], "narrow", mask)
    return held


def near(held, own=None):
    both = dict(held)
    for m in held:
        both[m ^ 1] = swap(held[m], "narrow", 1) if m or own is None else own
    return [both[m] for m in range(len(both))]


def tie(*trees):
    return lax.optimization_barrier(trees)


def lead_kernel(obs_ref, ens_ref, order_ref, lead_ref, mark_ref, sem):
    nob = obs_ref.shape[0]
    nblk = mark_ref.shape[0]

    for i in range(nblk):
        mark_ref[i] = 0
    place = 0
    for i in range(nob):
        block = obs_ref[i]
        order_ref[place] = block
        place = place + 1 - mark_ref[block]
        mark_ref[block] = 1
    for i in range(nblk):
        order_ref[place] = i
        place = place + 1 - mark_ref[i]
    copy_blocks(order_ref, 0, ens_ref, lead_ref, sem)
    wait_blocks(ens_ref, lead_ref, sem)


def copy_blocks(order_ref, first, ens_ref, out_ref, sem):
    count = out_ref.shape[1] // CLASSES

    def start(q, c):
        src = pl.multiple_of(order_ref[first + q] * CLASSES, CLASSES)
        dst = pl.multiple_of(q * CLASSES, CLASSES)
        pltpu.make_async_copy(
            ens_ref.at[:, pl.ds(src, CLASSES)], out_ref.at[:, pl.ds(dst, CLASSES)], sem
        ).start()
        return c

    lax.fori_loop(0, count, start, 0, unroll=4)


def wait_blocks(ens_ref, out_ref, sem):
    pltpu.make_async_copy(ens_ref.at[:, pl.ds(0, out_ref.shape[1])], out_ref, sem).wait()


def lead_blocks(obs_block, ensemble, lead):
    members, states = ensemble.shape
    nblk = states // CLASSES
    return pl.pallas_call(
        lead_kernel,
        out_shape=(
            jax.ShapeDtypeStruct((2 * nblk,), jnp.int32),
            jax.ShapeDtypeStruct((members, lead * CLASSES), BF16),
        ),
        in_specs=[SMEM, HBM],
        out_specs=(SMEM, VMEM),
        scratch_shapes=[pltpu.SMEM((nblk,), jnp.int32), pltpu.SemaphoreType.DMA],
        compiler_params=pltpu.CompilerParams(vmem_limit_bytes=50 * MIB),
        name="lead_blocks",
    )(obs_block, ensemble)


def rest_kernel(lead, order_ref, ens_ref, *refs):
    outs, sems = refs[:-1], refs[-1]
    first = lead
    for c, out in enumerate(outs):
        copy_blocks(order_ref, first, ens_ref, out, sems.at[c])
        first += out.shape[1] // CLASSES
    for c, out in enumerate(outs):
        wait_blocks(ens_ref, out, sems.at[c])


def rest_blocks(order, ensemble, lead, sizes):
    members = ensemble.shape[0]
    count = len(sizes)
    return pl.pallas_call(
        functools.partial(rest_kernel, lead),
        out_shape=[jax.ShapeDtypeStruct((members, n * CLASSES), BF16) for n in sizes],
        in_specs=[SMEM, HBM],
        out_specs=[VMEM] * count,
        scratch_shapes=[pltpu.SemaphoreType.DMA((count,))],
        compiler_params=pltpu.CompilerParams(vmem_limit_bytes=56 * MIB),
        name="rest_blocks",
    )(order, ensemble)


def split_rows(row, count, terms):
    ids = lax.broadcasted_iota(jnp.int32, (count, row.shape[1]), 0)
    out = jnp.zeros((count, row.shape[1]), F32)
    left = row
    for t in range(terms):
        part = left.astype(BF16).astype(F32)
        out = jnp.where(ids == t, part, out)
        left = left - part
    return out.astype(BF16)


def tail_of(rows, count):
    high = rows.astype(BF16).astype(F32)
    below = jnp.zeros((count - 2 * rows.shape[0], rows.shape[1]), F32)
    return jnp.concatenate([high, rows - high, below], axis=0).astype(BF16)


def rows_of_tail(tail):
    tail = tail.astype(F32)
    return tail[:8] + tail[8:16]


def slab_width(own, local):
    pairs = own * (own - 1) // 2 + own * own // 2
    return own * 3 // 2 * (local // 2) + pairs * local


def is_high(index_ref):
    return lax.rem(index_ref[0], 2) == 1


def gram_kernel(parts, scale_root, width, *refs):
    index_ref = refs[0]
    raws = refs[1 : parts + 1]
    factor_ref, weight_ref, root_ref, level_ref = refs[parts + 1 : parts + 5]
    keep_one, send_one, keep_two, send_two, halves, scaled, own, pulls = refs[parts + 5 :]
    local, cols = raws[0].shape
    half = local // 2
    count = parts // 2
    for first in range(0, cols, width):
        part = slice(first, first + width)
        factor = factor_ref[:, part]
        mean = column_sums([r[:, part] for r in raws]) / (local * parts)
        both = factor * root_ref[:, part]
        for m, r in enumerate(raws):
            v = r[:, part].astype(F32) - mean
            place = (m % 2 * count + m // 2) * local
            scaled[place : place + local, part] = (both * v).astype(BF16)
            if m % 2 == 0:
                own[m // 2 * local : (m // 2 + 1) * local, part] = (factor * v).astype(BF16)
        pull = level_ref[:, part] - mean * weight_ref[:, part] * scale_root
        pulls[:, part] = split_rows(pull, PAD, 3)

    high = is_high(index_ref)
    at = [0, 0]

    def put(which, value):
        halves[which, :, at[which] : at[which] + value.shape[1]] = value.astype(BF16)
        at[which] += value.shape[1]

    side = count * local
    blocks = {}
    for j in range(count):
        product = dot_nt(scaled[j * local : side, :], scaled[j * local : (j + 1) * local, :])
        for i in range(j, count):
            blocks[i, j] = product[(i - j) * local : (i - j + 1) * local]
    for i in range(count):
        put(i % 2, blocks[i, i][:half, :half])
        put(1 - i % 2, blocks[i, i][half:, :])
    for i in range(count):
        for j in range(i):
            put(0, blocks[i, j][:half])
            put(1, blocks[i, j][half:])
    low = scaled[pl.ds(pl.multiple_of(jnp.where(high, side, 0), side), side), :]
    for c in range(count // 2):
        first = jnp.where(high, (c + count // 2) * local, side + c * local)
        product = dot_nt(low, scaled[pl.ds(pl.multiple_of(first, local), local), :])
        for i in range(count):
            blocks[i, c] = product[i * local : (i + 1) * local]
    for i in range(count):
        for c in range(count // 2):
            put(0, blocks[i, c][:half])
            put(1, blocks[i, c][half:])
    row = jnp.sum(dot_nt(pulls[...], own[...]), axis=0, keepdims=True)
    ids = lax.broadcasted_iota(jnp.int32, (8, LANES), 0)
    rows = jnp.zeros((8, LANES), F32)
    for r in range(side // LANES):
        rows = jnp.where(ids == r, row[:, r * LANES : (r + 1) * LANES], rows)
    quarter = half // 2
    across = halves.shape[2]
    mine = pl.multiple_of(index_ref[1] * quarter, quarter)
    other = pl.multiple_of((1 - index_ref[1]) * quarter, quarter)
    for ref, which, first in (
        (keep_one, 0, mine),
        (send_one, 0, other),
        (keep_two, 1, mine),
        (send_two, 1, other),
    ):
        ref[:, :across] = halves[which, pl.ds(first, quarter), :]
        if which == 0:
            ref[:, across:] = tail_of(rows, quarter)


def gram_rows(index, raws, factor, weight, root, level, scale_root, width=256):
    parts = len(raws)
    local, cols = raws[0].shape
    half = local // 2
    members = local * parts
    across = slab_width(parts // 2, local)
    return pl.pallas_call(
        functools.partial(gram_kernel, parts, scale_root, width),
        out_shape=(
            jax.ShapeDtypeStruct((half // 2, across + LANES), BF16),
            jax.ShapeDtypeStruct((half // 2, across + LANES), BF16),
            jax.ShapeDtypeStruct((half // 2, across), BF16),
            jax.ShapeDtypeStruct((half // 2, across), BF16),
        ),
        in_specs=[SMEM] + [VMEM] * (parts + 4),
        out_specs=(VMEM, VMEM, VMEM, VMEM),
        scratch_shapes=[
            pltpu.VMEM((2, half, across), BF16),
            pltpu.VMEM((members, cols), BF16),
            pltpu.VMEM((members // 2, cols), BF16),
            pltpu.VMEM((PAD, cols), BF16),
        ],
        compiler_params=pltpu.CompilerParams(vmem_limit_bytes=24 * MIB),
        cost_estimate=pl.CostEstimate(flops=1024, bytes_accessed=1024, transcendentals=0),
        name="gram_rows",
    )(index, *raws, factor, weight, root, level)


def add_kernel(across, a_ref, b_ref, out_ref):
    both = a_ref[:, :across].astype(F32) + b_ref[:, :across].astype(F32)
    out_ref[:, :across] = both.astype(BF16)
    if across < a_ref.shape[1]:
        rows = rows_of_tail(a_ref[:, across:]) + rows_of_tail(b_ref[:, across:])
        out_ref[:, across:] = tail_of(rows, a_ref.shape[0])


def add_slabs(a, b, across):
    return pl.pallas_call(
        functools.partial(add_kernel, across),
        out_shape=jax.ShapeDtypeStruct(a.shape, BF16),
        in_specs=[VMEM, VMEM],
        out_specs=VMEM,
        compiler_params=pltpu.CompilerParams(vmem_limit_bytes=16 * MIB),
        name="add_slabs",
    )(a, b)


def join_kernel(index_ref, one_ref, other_one_ref, two_ref, other_two_ref, out_ref):
    quarter, across = two_ref.shape
    mine = pl.multiple_of(index_ref[1] * quarter, quarter)
    other = pl.multiple_of((1 - index_ref[1]) * quarter, quarter)
    out_ref[pl.ds(mine, quarter), :across] = one_ref[:, :across]
    out_ref[pl.ds(other, quarter), :across] = other_one_ref[:, :across]
    out_ref[pl.ds(2 * quarter + mine, quarter), :across] = two_ref[...]
    out_ref[pl.ds(2 * quarter + other, quarter), :across] = other_two_ref[...]
    out_ref[:quarter, across:] = one_ref[:, across:]
    out_ref[quarter:, across:] = jnp.zeros((3 * quarter, out_ref.shape[1] - across), BF16)


def join_slabs(index, one, other_one, two, other_two):
    quarter = two.shape[0]
    return pl.pallas_call(
        join_kernel,
        out_shape=jax.ShapeDtypeStruct((4 * quarter, one.shape[1]), BF16),
        in_specs=[SMEM] + [VMEM] * 4,
        out_specs=VMEM,
        compiler_params=pltpu.CompilerParams(vmem_limit_bytes=16 * MIB),
        name="join_slabs",
    )(index, one, other_one, two, other_two)


def root_kernel(parts, scale_root, tile, *refs):
    index_ref, mine_ref, sibling_ref, out_ref, sums_ref = refs[:5]
    u, ub, rest, rb, wb, wb2, tail = refs[5:]
    members = u.shape[0]
    local = members // parts
    half = local // 2
    count = parts // 2
    diag = lax.broadcasted_iota(jnp.int32, (local, local), 0) == lax.broadcasted_iota(
        jnp.int32, (local, local), 1
    )
    square = jnp.zeros((1, members), F32)

    def span(m):
        return slice(m * local, (m + 1) * local)

    def put_pair(i, j, block):
        u[span(i), span(j)] = block
        u[span(j), span(i)] = block.T

    high = is_high(index_ref)
    crossed = []
    for side, slab in enumerate((mine_ref, sibling_ref)):
        at = [0, 0]

        def take(which, width):
            first = at[which]
            at[which] += width
            return slab[which * half : (which + 1) * half, first : first + width].astype(F32)

        for i in range(count):
            corner = take(i % 2, half)
            lower = take(1 - i % 2, local)
            upper = jnp.concatenate([corner, lower[:, :half].T], axis=1)
            block = jnp.concatenate([upper, lower], axis=0) + jnp.where(diag, 1.0, 0.0)
            u[span(2 * i + side), span(2 * i + side)] = block
        for i in range(count):
            for j in range(i):
                block = jnp.concatenate([take(0, local), take(1, local)], axis=0)
                put_pair(2 * i + side, 2 * j + side, block)
        for i in range(count):
            for c in range(count // 2):
                block = jnp.concatenate([take(0, local), take(1, local)], axis=0)
                crossed.append((side, i, c, block))
    for side, i, c, block in crossed:

        @pl.when(high)
        def _():
            put_pair(2 * i + 1, 2 * (c + (1 - side) * (count // 2)), block)

        @pl.when(jnp.logical_not(high))
        def _():
            put_pair(2 * i, 2 * (c + side * (count // 2)) + 1, block)

    for m in range(parts):
        part = u[m * local : (m + 1) * local, :]
        square = square + jnp.sum(part * part, axis=0, keepdims=True)
    frob = jnp.sqrt(jnp.sum(square, axis=1, keepdims=True))

    def each_column(body):
        for first in range(0, members, tile):
            body(slice(first, members), slice(first, first + tile))

    def mirror(ref, below, col, value):
        value = value.astype(BF16)
        ref[below, col] = value
        for first in range(col.stop, members, tile):
            block = value[first - col.start : first - col.start + tile]
            ref[col, first : first + tile] = block.T

    inverse = 1.0 / frob
    ub[:members, :] = (u[...] * inverse).astype(BF16)

    def square_columns(below, col):
        v = dot(ub[below, :], ub[:members, col])
        unit = u[below, col] * inverse
        mirror(wb, below, col, v)
        mirror(wb2, below, col, 0.0625 * v - 0.5625 * unit)
        rest[below, col] = 1.6875 * v - 2.4375 * unit

    def second_columns(below, col):
        r = rest[below, col] + dot(wb[below, :], wb2[:, col])
        rest[below, col] = r
        mirror(rb, below, col, r)

    each_column(square_columns)
    each_column(second_columns)

    sums = []
    for slab in (mine_ref, sibling_ref):
        rows = rows_of_tail(slab[:PAD, slab.shape[1] - LANES :])
        pieces = [rows[r : r + 1, :] for r in range(count * local // LANES)]
        sums.append(jnp.concatenate(pieces, axis=1))
    projected = jnp.concatenate(
        [sums[m % 2][:, m // 2 * local : (m // 2 + 1) * local] for m in range(parts)], axis=1
    )
    ub[members:, :] = split_rows(projected, PAD, 2)

    def z_columns(below, col):
        y = dot(ub[below.start :, :], rb[:members, col])
        z = (2.25 * inverse) * u[below, col] + y[:-PAD]
        tail[:, col] = y[-PAD:]
        mirror(wb, below, col, z)

    def a_columns(below, col):
        a = 2.25 * wb[below, col].astype(F32) + dot(wb[below, :], rb[:members, col])
        mirror(wb2, below, col, a)
        rest[below, col] = 1.5 * rest[below, col] - 1.125 * a

    def third_columns(below, col):
        y = dot(rb[below.start :, :], wb2[:, col])
        r = rest[below, col] - 0.5 * y[:-PAD]
        tail[:, col] = y[-PAD:]
        rest[below, col] = r
        mirror(wb, below, col, r)

    each_column(z_columns)
    second_row = 2.25 * projected + jnp.sum(tail[...], axis=0, keepdims=True)
    rb[members:, :] = split_rows(second_row, PAD, 2)
    each_column(a_columns)
    each_column(third_columns)
    third_row = 1.5 * second_row - 0.5 * jnp.sum(tail[...], axis=0, keepdims=True)
    rest_rows = rest[:, :local].T

    def times(slab, row, mat):
        y = dot(jnp.concatenate([slab.astype(BF16), split_rows(row, PAD, 2)], axis=0), mat)
        return y[:local], jnp.sum(y[local:], axis=0, keepdims=True)

    def row_times(row, mat):
        return jnp.sum(dot(split_rows(row, PAD, 2), mat), axis=0, keepdims=True)

    unit_cols = ub[:members, :]
    rest_cols = wb[...]
    y, z_row = times(rest_rows, third_row, unit_cols)
    z = (3.375 * inverse) * u[:local, :] + y
    y, a_row = times(z, z_row, rest_cols)
    a, a_row = 3.375 * z + y, 3.375 * z_row + a_row
    y, b_row = times(a, a_row, rest_cols)
    b, b_row = 3.375 * a + y, 3.375 * a_row + b_row
    eye = jnp.concatenate(
        [jnp.where(diag, 3.375, 0.0), jnp.zeros((local, members - local), F32)], axis=1
    )
    fourth = 1.5 * (eye + rest_rows) - 0.5 * b
    midway = 1.5 * third_row - 0.5 * b_row
    y_row = 3.375 * midway + row_times(midway, rest_cols)
    z_row = row_times(y_row, unit_cols)
    a_row = 3.375 * z_row + row_times(z_row, rest_cols)
    b_row = 3.375 * a_row + row_times(a_row, rest_cols)
    shift = (1.5 * y_row - 0.5 * b_row) * (inverse / scale_root)
    transform = (fourth * jnp.sqrt(inverse) + shift).astype(BF16)
    out_ref[...] = transform
    row_sums = jnp.sum(transform.astype(F32), axis=1, keepdims=True)
    sums_ref[...] = jnp.broadcast_to(row_sums, sums_ref.shape)


def transform_rows(index, mine, sibling, parts, scale_root, tile=256):
    local = mine.shape[0]
    members = local * parts
    wide = pltpu.VMEM((members, members), F32)
    narrow = pltpu.VMEM((members, members), BF16)
    longer = pltpu.VMEM((members + PAD, members), BF16)
    return pl.pallas_call(
        functools.partial(root_kernel, parts, scale_root, tile),
        out_shape=(
            jax.ShapeDtypeStruct((local, members), BF16),
            jax.ShapeDtypeStruct((local, LANES), F32),
        ),
        in_specs=[SMEM] + [VMEM] * 2,
        out_specs=(VMEM, VMEM),
        scratch_shapes=[wide, longer, wide, longer, narrow, narrow]
        + [pltpu.VMEM((PAD, members), F32)],
        compiler_params=pltpu.CompilerParams(vmem_limit_bytes=36 * MIB),
        cost_estimate=pl.CostEstimate(flops=1024, bytes_accessed=1024, transcendentals=0),
        name="transform_rows",
    )(index, mine, sibling)


def sums_kernel(width, *refs):
    out_ref = refs[-1]
    for first in range(0, out_ref.shape[1], width):
        part = slice(first, min(first + width, out_ref.shape[1]))
        out_ref[:, part] = column_sums([r[:, part] for r in refs[:-1]])


def column_sums(pieces):
    total = jnp.sum(pieces[0].astype(F32), axis=0, keepdims=True)
    for piece in pieces[1:]:
        total = total + jnp.sum(piece.astype(F32), axis=0, keepdims=True)
    return total


def sums(pieces, width=256):
    return pl.pallas_call(
        functools.partial(sums_kernel, width),
        out_shape=jax.ShapeDtypeStruct((1, pieces[0].shape[1]), F32),
        in_specs=[VMEM] * len(pieces),
        out_specs=VMEM,
        compiler_params=pltpu.CompilerParams(vmem_limit_bytes=16 * MIB),
        cost_estimate=pl.CostEstimate(flops=1024, bytes_accessed=1024, transcendentals=0),
        name="sums",
    )(*pieces)


def update_kernel(width, parts, start, summed, order_ref, t_ref, rows_ref, factor_ref, *refs):
    raws, totals = refs[: parts * len(summed)], refs[parts * len(summed) : (parts + 1) * len(summed)]
    out_ref, buf, sem = refs[-3:]
    local, members = t_ref.shape
    rows = rows_ref[:, :1]
    col = 0
    for chunk, (done, total_ref) in enumerate(zip(summed, totals)):
        held = raws[chunk * parts : (chunk + 1) * parts]
        for first in range(0, held[0].shape[1], width):
            count = min(width, held[0].shape[1] - first)
            part = slice(first, first + count)
            pieces = [r[:, part] for r in held]
            total = total_ref[:, part]
            if done < parts:
                total = total + column_sums(pieces[done:])
            mean = total / members
            factor = factor_ref[:, start + col : start + col + count]
            product = dot(t_ref[:, :local], held[0][:, part])
            for m in range(1, parts):
                product += dot(t_ref[:, m * local : (m + 1) * local], held[m][:, part])
            buf[:, col : col + count] = (
                factor * product + (mean - (mean * factor) * rows)
            ).astype(BF16)
            for q in range(0, count, CLASSES):
                src = col + q
                dst = pl.multiple_of(order_ref[(start + src) // CLASSES] * CLASSES, CLASSES)
                pltpu.make_async_copy(
                    buf.at[:, pl.ds(src, CLASSES)], out_ref.at[:, pl.ds(dst, CLASSES)], sem
                ).start()
            col += count
    pltpu.make_async_copy(buf, out_ref.at[:, pl.ds(0, col)], sem).wait()


def update(order, transform, factor, chunks, totals, summed, start, result=None, width=1024):
    local = transform[0].shape[0]
    parts = len(chunks[0])
    states = factor.shape[1]
    cols = sum(raws[0].shape[1] for raws in chunks)
    raws = [x for held in chunks for x in held]
    extra = [] if result is None else [result]
    inputs = raws + totals
    return pl.pallas_call(
        functools.partial(update_kernel, width, parts, start, summed),
        out_shape=jax.ShapeDtypeStruct((local, states), BF16),
        in_specs=[SMEM, VMEM, VMEM, VMEM] + [VMEM] * len(inputs) + [ANY] * len(extra),
        out_specs=ANY,
        scratch_shapes=[pltpu.VMEM((local, cols), BF16), pltpu.SemaphoreType.DMA],
        input_output_aliases={4 + len(inputs): 0} if extra else {},
        compiler_params=pltpu.CompilerParams(vmem_limit_bytes=24 * MIB),
        cost_estimate=pl.CostEstimate(flops=1024, bytes_accessed=1024, transcendentals=0),
        name="update",
    )(order, *transform, factor, *inputs, *extra)


def on_device(ensemble, owner, inflation, obs_block, obs_value, obs_std):
    local, states = ensemble.shape
    parts = lax.axis_size("narrow")
    members = local * parts
    nblk = states // CLASSES
    nob = obs_block.shape[0]
    scale_root = math.sqrt(members - 1)

    order, lead = lead_blocks(obs_block, ensemble, nob)
    lead_far = far(lead)
    left = nblk - nob
    sizes = [left * 33 // 48]
    sizes.append(left - sum(sizes))
    starts = [nob * CLASSES]
    for n in sizes[:-1]:
        starts.append(starts[-1] + n * CLASSES)
    rest = list(rest_blocks(order, ensemble, nob, sizes))

    pick = order[:nblk, None] == jnp.arange(nblk, dtype=jnp.int32)[None, :]
    owner_new = jnp.sum(jnp.where(pick, owner[None, :], 0), axis=1)
    comps = jnp.arange(inflation.shape[0], dtype=jnp.int32)
    factor_new = jnp.sum(
        jnp.where(owner_new[:, None] == comps[None, :], inflation[None, :], 0.0), axis=1
    )
    factor = jnp.repeat(factor_new, CLASSES).reshape(1, states)
    match = (order[:nob, None] == obs_block[None, :])[:, :, None]
    inverse = 1.0 / (obs_std * obs_std)
    weight = jnp.sum(jnp.where(match, inverse.reshape(1, nob, CLASSES), 0.0), axis=1)
    weight = weight.reshape(1, nob * CLASSES) / (members - 1)
    level = jnp.sum(jnp.where(match, (obs_value * inverse).reshape(1, nob, CLASSES), 0.0), axis=1)
    level = level.reshape(1, nob * CLASSES) / scale_root

    root = jnp.sqrt(weight)
    index = jnp.stack([lax.axis_index("narrow"), lax.rem(lax.axis_index("wide"), 2)])
    fars = [far(chunk) for chunk in rest]
    owns = [swap(chunk, "narrow", 1) for chunk in rest]
    lead_far, lead_own, rest, factor, weight, root, level = tie(
        lead_far, swap(lead, "narrow", 1), rest, factor, weight, root, level
    )
    lead_all = near(lead_far, lead_own)
    one, send_one, two, send_two = gram_rows(
        index, lead_all, factor, weight, root, level, scale_root
    )

    across = two.shape[1]
    masks = masks_of(lax.axis_size("wide"))
    steps = masks + [1]
    for slot in range(len(steps) + 1):
        one, two, send_one, send_two = tie(one, two, send_one, send_two)
        got = []
        if slot < len(steps):
            got.append(swap(send_one if slot == 0 else one, "wide", steps[slot]))
        if slot > 0:
            got.append(swap(send_two if slot == 1 else two, "wide", steps[slot - 1]))
        if slot == 0:
            total = sums(lead_all)
            got, total = tie(got, total)
        elif slot == 1:
            early = [sums([chunk, own]) for chunk, own in zip(rest, owns)]
            got, early, owns = tie(got, early, owns)
        elif slot == len(steps):
            got, fars[0] = tie(got, fars[0])
        else:
            (got,) = tie(got)
        if slot < len(masks):
            one = add_slabs(one, got[0], across)
        elif slot == len(masks):
            other_one = got[0]
        if 0 < slot <= len(masks):
            two = add_slabs(two, got[-1], across)
        elif slot > len(masks):
            other_two = got[-1]
    slab = join_slabs(index, one, other_one, two, other_two)
    sibling, all_one = tie(swap(slab, "narrow", 1), near(fars[0], owns[0]))
    transform = transform_rows(index, slab, sibling, parts, scale_root)
    result = update(order, transform, factor, [all_one], [early[0]], [2], starts[0])
    fars[1], result = tie(fars[1], result)
    all_two = near(fars[1], owns[1])
    result = update(order, transform, factor, [lead_all], [total], [parts], 0, result)
    return update(order, transform, factor, [all_two], [early[1]], [2], starts[1], result)


def solution(mesh):
    return jax.shard_map(
        on_device,
        mesh=mesh,
        in_specs=(P("narrow", "wide"), P("wide"), P(), P("wide"), P("wide"), P("wide")),
        out_specs=P("narrow", "wide"),
        check_vma=False,
    )
```
